512 devices in a mesh: ctx: 32 (over x, y), rep: 8 (over z), fsdp: 2 (over core).
Axes of the slice: x: 4, y: 8, z: 8, core: 2. Of those that a mesh axis runs over, the one named last changes fastest.
Arguments:
- values: bfloat16 [8, 4096, 2048], P('rep', 'ctx', 'fsdp'), may hold values from -6 to 6
- gates: bfloat16 [8, 4096, 2048], P('rep', 'ctx', 'fsdp'), may hold values from -6 to 6
- skip_gain: float32 [2048], P('fsdp'), may hold values from -4 to 4
- filter_taps: float32 [4096, 2048], P('ctx', 'fsdp'), may hold values from -8 to 8
- out_weight: bfloat16 [2048, 4096], P('fsdp', 'rep'), may hold values from -0.125 to 0.125
Outputs:
- output: bfloat16 [8, 4096, 4096], P(None, 'ctx', ('rep', 'fsdp'))
The draws below stay inside these ranges and needn't reach their ends.
All inputs are finite; a program needn't handle non-finite values.
Results may differ from the reference program's by a relative error of at most 0.0049.
Values may be sent and summed in bfloat16 or wider, within the bound.
No kernel may reach another device: no remote copies, remote signals or barrier semaphores. Data moves between devices by JAX's collectives and lax.ppermute only.
A program may use at most 128 MiB of HBM per device.

```python
import math
import jax
import jax.numpy as jnp
from jax import lax

D = 4096
DC = 2048
SPAN = 4096
SEQS = 8


def draw_filter_taps(key, part):
    key = jax.random.fold_in(key, 7)
    rough_key = jax.random.fold_in(key, 1)
    rate_key = jax.random.fold_in(key, 2)
    lags = jnp.arange(SPAN, dtype=jnp.float32)[:, None]
    log_tau = jax.random.uniform(rate_key, (DC,), jnp.float32, math.log(30.0), math.log(4.0 * SPAN))
    tau = jnp.exp(log_tau)[None, :]
    envelope = jnp.exp(-lags / tau)
    ratio = jnp.exp(-2.0 / tau)
    whole = jnp.exp(-2.0 * SPAN / tau)
    scale_term = jnp.sqrt((1.0 - ratio) / (1.0 - whole))
    rough = jnp.clip(jax.random.normal(rough_key, (SPAN, DC), jnp.float32), -5.0, 5.0)
    return (rough * envelope * scale_term).astype(jnp.float32)


def steps_of(own_key, dims, cuts, smallest, high):
    def one(position, blocks):
        steps = jax.random.uniform(jax.random.fold_in(jax.random.fold_in(own_key, 6), position), (blocks,), jnp.float32, smallest / len(cuts), high / len(cuts))
        return jnp.repeat(jnp.exp(steps), dims[position] // blocks).reshape((-1,) + (1,) * (len(dims) - position - 1))

    factor_of = one(*cuts[0])
    for cut in cuts[1:]:
        factor_of = factor_of * one(*cut)
    return factor_of


def bell_draw(rng, shape, spread, limit, split=(), kind=jnp.bfloat16):
    values = jax.random.normal(rng, shape, jnp.float32) * spread
    if len(split) > 0:
        values = steps_of(rng, shape, split, -0.22, 0.18) * values
    return jnp.clip(values, min=-limit, max=limit).astype(kind)


def setup_inputs(seed: int = 0) -> dict:
    keys = jax.random.split(jax.random.key(seed), 6)
    return {
        "values": bell_draw(keys[0], (SEQS, SPAN, DC), 1.0, 6.0, ((0, 8), (1, 32), (2, 2))),
        "gates": bell_draw(keys[1], (SEQS, SPAN, DC), 1.0, 6.0, ((0, 8), (1, 32), (2, 2))),
        "skip_gain": bell_draw(keys[2], (DC,), 1.0, 4.0, ((0, 2),), jnp.float32),
        "filter_taps": draw_filter_taps(jax.random.fold_in(keys[5], 71), 0),
        "out_weight": bell_draw(keys[4], (DC, D), DC ** -0.5, 0.125, ((0, 2), (1, 8))),
    }


def reference(values, gates, skip_gain, filter_taps, out_weight):
    double_len = 2 * SPAN
    filter_spec = jnp.fft.rfft(filter_taps, n=double_len, axis=0)

    def project_one(inputs):
        seq_vals, seq_gates = inputs
        as_float = seq_vals.astype(jnp.float32)
        spectrum = jnp.fft.rfft(as_float, n=double_len, axis=0) * filter_spec
        convolved = jnp.fft.irfft(spectrum, n=double_len, axis=0)[:SPAN].astype(jnp.float32)
        mixed = (seq_gates.astype(jnp.float32) * (convolved + skip_gain[None, :] * as_float)).astype(jnp.bfloat16)
        return jnp.dot(mixed, out_weight, preferred_element_type=jnp.float32).astype(jnp.bfloat16)

    return lax.map(project_one, (values, gates))
```

```python
import math

import jax
import jax.numpy as jnp
import ml_dtypes
import numpy as np
from jax import lax
from jax.experimental import pallas as pl
from jax.experimental.pallas import tpu as pltpu
from jax.sharding import PartitionSpec as P

F32, BF16 = jnp.float32, jnp.bfloat16


def two_parts(table):
    high = table.astype(ml_dtypes.bfloat16)
    low = (table - high.astype(np.float64)).astype(ml_dtypes.bfloat16)
    return high, low


def dft_tables(block):
    points = 2 * block
    angle = 2.0 * math.pi / points * (np.arange(block) + 0.5)[None, :] * np.arange(points)[:, None]
    forward = np.concatenate([np.cos(angle), -np.sin(angle)], axis=1)[:block]
    inverse = np.concatenate([np.cos(angle), -np.sin(angle)], axis=1).T * (2.0 / points)
    return np.concatenate(two_parts(forward), axis=0), np.stack(two_parts(inverse))


def pack_kernel(values_ref, taps_ref, out_ref):
    peers, rows, block = out_ref.shape
    width = rows // 2
    for first, source in ((0, values_ref), (width, taps_ref)):
        turned = source[...].astype(F32).T.astype(BF16)
        out_ref[:, first : first + width, :] = turned.reshape(peers, width, block)


def conv_kernel(in_ref, fwd_ref, inv_ref, out_ref, src, lag, spec):
    count, rows, block = in_ref.shape
    width = rows // 2
    for first, dest in ((0, src), (width, lag)):
        part = in_ref[:, first : first + width, :].reshape(count * width, block)
        both = jnp.concatenate([part, part], axis=1)
        wave = jnp.dot(both, fwd_ref[...], preferred_element_type=F32)
        real = wave[:, :block].reshape(count, width, block)
        imag = wave[:, block:].reshape(count, width, block)
        dest[0] = real
        dest[1] = imag
        dest[2] = real + imag

    group = 4

    def some_channels(step, carry):
        here = pl.ds(pl.multiple_of(step * 8, 8), 8)
        for i0 in range(0, count, group):
            sums = [[None] * 3 for _ in range(group)]
            for j0 in range(0, i0 + group, group):
                for p in range(3):
                    taps = {k: lag[p, k, here, :] for k in range(max(i0 - j0 - group + 1, 0), i0 - j0 + group)}
                    for dj in range(group):
                        source = src[p, j0 + dj, here, :]
                        for di in range(group):
                            k = i0 + di - j0 - dj
                            if k >= 0:
                                term = source * taps[k]
                                sums[di][p] = term if sums[di][p] is None else sums[di][p] + term
            for di in range(group):
                rr, ii, ss = sums[di]
                spec[i0 + di, here, :block] = rr - ii
                spec[i0 + di, here, block:] = ss - rr - ii
        return carry

    lax.fori_loop(0, width // 8, some_channels, 0)
    whole = spec[...].reshape(count * width, 2 * block)
    high = whole.astype(BF16)
    low = (whole - high.astype(F32)).astype(BF16)
    wide = (
        jnp.dot(high, inv_ref[0], preferred_element_type=F32)
        + jnp.dot(low, inv_ref[0], preferred_element_type=F32)
        + jnp.dot(high, inv_ref[1], preferred_element_type=F32)
    )
    head = wide[:, :block].reshape(count, width, block)
    tail = wide[:, block:].reshape(count, width, block)
    out_ref[0] = head[0].astype(BF16)
    out_ref[1:] = (head[1:] + tail[:-1]).astype(BF16)


def gate_kernel(conv_ref, values_ref, gates_ref, gain_ref, out_ref):
    peers, width, block = conv_ref.shape
    convolved = conv_ref[...].reshape(peers * width, block).astype(F32).T
    direct = gain_ref[...] * values_ref[...].astype(F32)
    out_ref[...] = (gates_ref[...].astype(F32) * (convolved + direct)).astype(BF16)


def place_kernel(place_ref, own_a, own_b, got_a, out_ref):
    mine = place_ref[0]
    seqs, block, _ = out_ref.shape
    odd = mine % 2
    even_chip = mine + odd
    odd_chip = even_chip - 1
    near_mine = jnp.where(odd == 1, odd_chip - 1, even_chip)
    near_theirs = jnp.where(odd == 1, even_chip, odd_chip - 1)
    far_mine = jnp.where(odd == 1, mine - 3, mine + 2)
    for part, first, second in (
        (own_a, near_mine, near_mine + 1),
        (got_a, near_theirs, near_theirs + 1),
        (own_b, far_mine, far_mine + 1),
    ):
        out_ref[lax.rem(first + 2 * seqs, seqs)] = part[:block]
        out_ref[lax.rem(second + 2 * seqs, seqs)] = part[block:]


def place_most(place, own_a, own_b, got_a, seqs, block):
    return pl.pallas_call(
        place_kernel,
        in_specs=[pl.BlockSpec(memory_space=pltpu.SMEM)] + [pl.BlockSpec(memory_space=pltpu.VMEM)] * 3,
        out_shape=jax.ShapeDtypeStruct((seqs, block, own_a.shape[1]), BF16),
        name="place",
    )(place, own_a, own_b, got_a)


def body(values, gates, skip_gain, filter_taps, out_weight):
    block, chans = values.shape[1:]
    peers = lax.axis_size("ctx")
    width = chans // peers
    values, gates = values[0], gates[0]
    forward, inverse = dft_tables(block)
    count = lax.axis_size("rep")
    mine, core = lax.axis_index("rep"), lax.axis_index("fsdp")
    place = jnp.stack([mine, core]).astype(jnp.int32)
    row_pairs = [[i, i + 1] for i in range(0, count, 2)]
    column_swap = [(i, (i - 1 if i % 2 == 0 else i + 1) % count) for i in range(count)]
    onward = [(i, (i - 2 if i % 2 == 0 else i + 2) % count) for i in range(count)]
    partner_weight = lax.ppermute(out_weight, "rep", column_swap)

    packed = pl.pallas_call(
        pack_kernel, out_shape=jax.ShapeDtypeStruct((peers, 2 * width, block), BF16), name="pack"
    )(values, filter_taps)
    turned = lax.all_to_all(packed, "ctx", split_axis=0, concat_axis=0, tiled=True)
    convolved = pl.pallas_call(
        conv_kernel,
        out_shape=jax.ShapeDtypeStruct((peers, width, block), BF16),
        scratch_shapes=[
            pltpu.VMEM((3, peers, width, block), F32),
            pltpu.VMEM((3, peers, width, block), F32),
            pltpu.VMEM((peers, width, 2 * block), F32),
        ],
        compiler_params=pltpu.CompilerParams(vmem_limit_bytes=40 * 2**20),
        name="conv",
    )(turned, forward, inverse)
    back = lax.all_to_all(convolved, "ctx", split_axis=0, concat_axis=0, tiled=True)
    mixed = pl.pallas_call(
        gate_kernel, out_shape=jax.ShapeDtypeStruct((block, chans), BF16), name="gate"
    )(back, values, gates, skip_gain[None, :])

    keep = out_weight.shape[1] // 2
    weights = jnp.concatenate(
        [
            lax.dynamic_slice_in_dim(w, side * keep, keep, 1)
            for side in (core, 1 - core)
            for w in (out_weight, partner_weight)
        ],
        axis=1,
    )
    near = lax.all_gather(mixed, "rep", axis=0, axis_index_groups=row_pairs)
    far = lax.ppermute(near, "rep", onward)

    def columns(product):
        came = lax.all_gather(product[:, 2 * keep :].astype(BF16), "fsdp", axis=0)
        total = product[:, : 2 * keep] + lax.dynamic_index_in_dim(came, 1 - core, 0, False).astype(F32)
        total = total.astype(BF16)
        return total[:, :keep], lax.ppermute(total[:, keep:], "rep", column_swap)

    own_a, got_a = columns(
        jnp.dot(near.reshape(2 * block, chans), weights, preferred_element_type=F32)
    )
    far, own_a = lax.optimization_barrier((far, own_a))
    own_b, got_b = columns(
        jnp.dot(far.reshape(2 * block, chans), weights, preferred_element_type=F32)
    )
    out = place_most(place, own_a, own_b, got_a, count, block)
    low = jnp.where(mine % 2 == 1, mine + 3, mine - 4 + count) % count
    return lax.dynamic_update_slice(out, got_b.reshape(2, block, keep), (low, 0, 0))


def solution(mesh):
    return jax.shard_map(
        body,
        mesh=mesh,
        in_specs=(
            P("rep", "ctx", "fsdp"),
            P("rep", "ctx", "fsdp"),
            P("fsdp"),
            P("ctx", "fsdp"),
            P("fsdp", "rep"),
        ),
        out_specs=P(None, "ctx", ("rep", "fsdp")),
        check_vma=False,
    )
```

```python
import math

import jax
import jax.numpy as jnp
import ml_dtypes
import numpy as np
from jax import lax
from jax.experimental import pallas as pl
from jax.experimental.pallas import tpu as pltpu
from jax.sharding import PartitionSpec as P

F32, BF16 = jnp.float32, jnp.bfloat16


def two_parts(table):
    high = table.astype(ml_dtypes.bfloat16)
    low = (table - high.astype(np.float64)).astype(ml_dtypes.bfloat16)
    return high, low


def dft_tables(block):
    points = 2 * block
    angle = 2.0 * math.pi / points * (np.arange(block) + 0.5)[None, :] * np.arange(points)[:, None]
    forward = np.concatenate([np.cos(angle), -np.sin(angle)], axis=1)[:block]
    inverse = np.concatenate([np.cos(angle), -np.sin(angle)], axis=1).T * (2.0 / points)
    return np.concatenate(two_parts(forward), axis=0), np.stack(two_parts(inverse))


def pack_kernel(values_ref, taps_ref, out_ref, values, taps, arrived):
    peers, rows, block = out_ref.shape
    width = rows // 2
    parts = ((0, values_ref, values), (1, taps_ref, taps))
    copies = [pltpu.make_async_copy(source, here, arrived.at[n]) for n, source, here in parts]
    for copy in copies:
        copy.start()
    for n, _, here in parts:
        copies[n].wait()
        turned = here[...].astype(F32).T.astype(BF16)
        out_ref[:, n * width : (n + 1) * width, :] = turned.reshape(peers, width, block)


def conv_kernel(in_ref, fwd_ref, inv_ref, out_ref, src, lag, spec):
    count, rows, block = in_ref.shape
    width = rows // 2
    for first, dest in ((0, src), (width, lag)):
        part = in_ref[:, first : first + width, :].reshape(count * width, block)
        both = jnp.concatenate([part, part], axis=1)
        wave = jnp.dot(both, fwd_ref[...], preferred_element_type=F32)
        real = wave[:, :block].reshape(count, width, block)
        imag = wave[:, block:].reshape(count, width, block)
        dest[0] = real
        dest[1] = imag
        dest[2] = real + imag

    group = 4

    def some_channels(step, carry):
        here = pl.ds(pl.multiple_of(step * 8, 8), 8)
        for i0 in range(0, count, group):
            sums = [[None] * 3 for _ in range(group)]
            for j0 in range(0, i0 + group, group):
                for p in range(3):
                    taps = {k: lag[p, k, here, :] for k in range(max(i0 - j0 - group + 1, 0), i0 - j0 + group)}
                    for dj in range(group):
                        source = src[p, j0 + dj, here, :]
                        for di in range(group):
                            k = i0 + di - j0 - dj
                            if k >= 0:
                                term = source * taps[k]
                                sums[di][p] = term if sums[di][p] is None else sums[di][p] + term
            for di in range(group):
                rr, ii, ss = sums[di]
                spec[i0 + di, here, :block] = rr - ii
                spec[i0 + di, here, block:] = ss - rr - ii
        return carry

    lax.fori_loop(0, width // 8, some_channels, 0, unroll=True)
    whole = spec[...].reshape(count * width, 2 * block)
    high = whole.astype(BF16)
    low = (whole - high.astype(F32)).astype(BF16)
    wide = (
        jnp.dot(high, inv_ref[0], preferred_element_type=F32)
        + jnp.dot(low, inv_ref[0], preferred_element_type=F32)
        + jnp.dot(high, inv_ref[1], preferred_element_type=F32)
    )
    head = wide[:, :block].reshape(count, width, block)
    tail = wide[:, block:].reshape(count, width, block)
    out_ref[0] = head[0].astype(BF16)
    out_ref[1:] = (head[1:] + tail[:-1]).astype(BF16)


def gate_kernel(conv_ref, values_ref, gates_ref, gain_ref, out_ref):
    peers, width, block = conv_ref.shape
    convolved = conv_ref[...].reshape(peers * width, block).astype(F32).T
    direct = gain_ref[...] * values_ref[...].astype(F32)
    out_ref[...] = (gates_ref[...].astype(F32) * (convolved + direct)).astype(BF16)


def place_kernel(place_ref, own_a, own_b, got_a, out_ref):
    mine = place_ref[0]
    seqs, block, _ = out_ref.shape
    odd = mine % 2
    even_chip = mine + odd
    odd_chip = even_chip - 1
    near_mine = jnp.where(odd == 1, odd_chip - 1, even_chip)
    near_theirs = jnp.where(odd == 1, even_chip, odd_chip - 1)
    far_mine = jnp.where(odd == 1, mine - 3, mine + 2)
    for part, first, second in (
        (own_a, near_mine, near_mine + 1),
        (got_a, near_theirs, near_theirs + 1),
        (own_b, far_mine, far_mine + 1),
    ):
        out_ref[lax.rem(first + 2 * seqs, seqs)] = part[:block]
        out_ref[lax.rem(second + 2 * seqs, seqs)] = part[block:]


def place_most(place, own_a, own_b, got_a, seqs, block):
    return pl.pallas_call(
        place_kernel,
        in_specs=[pl.BlockSpec(memory_space=pltpu.SMEM)] + [pl.BlockSpec(memory_space=pltpu.VMEM)] * 3,
        out_shape=jax.ShapeDtypeStruct((seqs, block, own_a.shape[1]), BF16),
        compiler_params=pltpu.CompilerParams(vmem_limit_bytes=4 * 2**20),
        name="place",
    )(place, own_a, own_b, got_a)


def body(values, gates, skip_gain, filter_taps, out_weight):
    block, chans = values.shape[1:]
    peers = lax.axis_size("ctx")
    width = chans // peers
    values, gates = values[0], gates[0]
    forward, inverse = dft_tables(block)
    small = pltpu.CompilerParams(vmem_limit_bytes=8 * 2**20)
    count = lax.axis_size("rep")
    mine, core = lax.axis_index("rep"), lax.axis_index("fsdp")
    place = jnp.stack([mine, core]).astype(jnp.int32)
    row_pairs = [[i, i + 1] for i in range(0, count, 2)]
    column_swap = [(i, (i - 1 if i % 2 == 0 else i + 1) % count) for i in range(count)]
    onward = [(i, (i - 2 if i % 2 == 0 else i + 2) % count) for i in range(count)]
    partner_weight = lax.ppermute(out_weight, "rep", column_swap)

    packed = pl.pallas_call(
        pack_kernel,
        in_specs=[pl.BlockSpec(memory_space=pl.ANY)] * 2,
        out_shape=jax.ShapeDtypeStruct((peers, 2 * width, block), BF16),
        scratch_shapes=[
            pltpu.VMEM(values.shape, BF16),
            pltpu.VMEM(filter_taps.shape, F32),
            pltpu.SemaphoreType.DMA((2,)),
        ],
        compiler_params=pltpu.CompilerParams(vmem_limit_bytes=60 * 2**20),
        name="pack",
    )(values, filter_taps)
    turned = lax.all_to_all(packed, "ctx", split_axis=0, concat_axis=0, tiled=True)
    convolved = pl.pallas_call(
        conv_kernel,
        out_shape=jax.ShapeDtypeStruct((peers, width, block), BF16),
        scratch_shapes=[
            pltpu.VMEM((3, peers, width, block), F32),
            pltpu.VMEM((3, peers, width, block), F32),
            pltpu.VMEM((peers, width, 2 * block), F32),
        ],
        compiler_params=pltpu.CompilerParams(vmem_limit_bytes=20 * 2**20),
        name="conv",
    )(turned, forward, inverse)
    back = lax.all_to_all(convolved, "ctx", split_axis=0, concat_axis=0, tiled=True)
    mixed = pl.pallas_call(
        gate_kernel,
        out_shape=jax.ShapeDtypeStruct((block, chans), BF16),
        compiler_params=small,
        name="gate",
    )(back, values, gates, skip_gain[None, :])

    keep = out_weight.shape[1] // 2
    weights = jnp.concatenate(
        [
            lax.dynamic_slice_in_dim(w, side * keep, keep, 1)
            for side in (core, 1 - core)
            for w in (out_weight, partner_weight)
        ],
        axis=1,
    )
    near = lax.all_gather(mixed, "rep", axis=0, axis_index_groups=row_pairs)
    far = lax.ppermute(near, "rep", onward)

    def columns(product):
        came = lax.all_gather(product[:, 2 * keep :].astype(BF16), "fsdp", axis=0)
        total = product[:, : 2 * keep] + lax.dynamic_index_in_dim(came, 1 - core, 0, False).astype(F32)
        total = total.astype(BF16)
        return total[:, :keep], lax.ppermute(total[:, keep:], "rep", column_swap)

    own_a, got_a = columns(
        jnp.dot(near.reshape(2 * block, chans), weights, preferred_element_type=F32)
    )
    far, own_a = lax.optimization_barrier((far, own_a))
    own_b, got_b = columns(
        jnp.dot(far.reshape(2 * block, chans), weights, preferred_element_type=F32)
    )
    out = place_most(place, own_a, own_b, got_a, count, block)
    low = jnp.where(mine % 2 == 1, mine + 3, mine - 4 + count) % count
    return lax.dynamic_update_slice(out, got_b.reshape(2, block, keep), (low, 0, 0))


def solution(mesh):
    return jax.shard_map(
        body,
        mesh=mesh,
        in_specs=(
            P("rep", "ctx", "fsdp"),
            P("rep", "ctx", "fsdp"),
            P("fsdp"),
            P("ctx", "fsdp"),
            P("fsdp", "rep"),
        ),
        out_specs=P(None, "ctx", ("rep", "fsdp")),
        check_vma=False,
    )
```

```python
import math

import jax
import jax.numpy as jnp
import ml_dtypes
import numpy as np
from jax import lax
from jax.experimental import pallas as pl
from jax.experimental.pallas import tpu as pltpu
from jax.sharding import PartitionSpec as P

F32, BF16 = jnp.float32, jnp.bfloat16


def two_parts(table):
    high = table.astype(ml_dtypes.bfloat16)
    low = (table - high.astype(np.float64)).astype(ml_dtypes.bfloat16)
    return high, low


def dft_tables(block):
    points = 2 * block
    angle = 2.0 * math.pi / points * (np.arange(block) + 0.5)[None, :] * np.arange(points)[:, None]
    forward = np.concatenate([np.cos(angle), -np.sin(angle)], axis=1)[:block]
    inverse = np.concatenate([np.cos(angle), -np.sin(angle)], axis=1).T * (2.0 / points)
    return np.concatenate(two_parts(forward), axis=0), np.stack(two_parts(inverse))


def pack_kernel(values_ref, taps_ref, out_ref, values, taps, arrived):
    peers, rows, block = out_ref.shape
    width = rows // 2
    parts = ((0, values_ref, values), (1, taps_ref, taps))
    copies = [pltpu.make_async_copy(source, here, arrived.at[n]) for n, source, here in parts]
    for copy in copies:
        copy.start()
    for n, _, here in parts:
        copies[n].wait()
        turned = here[...].astype(F32).T.astype(BF16)
        out_ref[:, n * width : (n + 1) * width, :] = turned.reshape(peers, width, block)


def conv_kernel(in_ref, fwd_ref, inv_ref, out_ref, src, lag, spec):
    count, rows, block = in_ref.shape
    width = rows // 2
    for first, dest in ((0, src), (width, lag)):
        part = in_ref[:, first : first + width, :].reshape(count * width, block)
        both = jnp.concatenate([part, part], axis=1)
        wave = jnp.dot(both, fwd_ref[...], preferred_element_type=F32)
        real = wave[:, :block].reshape(count, width, block)
        imag = wave[:, block:].reshape(count, width, block)
        dest[0] = real
        dest[1] = imag
        dest[2] = real + imag

    group = 4

    def some_channels(step, carry):
        here = pl.ds(pl.multiple_of(step * 8, 8), 8)
        for i0 in range(0, count, group):
            sums = [[None] * 3 for _ in range(group)]
            for j0 in range(0, i0 + group, group):
                for p in range(3):
                    taps = {k: lag[p, k, here, :] for k in range(max(i0 - j0 - group + 1, 0), i0 - j0 + group)}
                    for dj in range(group):
                        source = src[p, j0 + dj, here, :]
                        for di in range(group):
                            k = i0 + di - j0 - dj
                            if k >= 0:
                                term = source * taps[k]
                                sums[di][p] = term if sums[di][p] is None else sums[di][p] + term
            for di in range(group):
                rr, ii, ss = sums[di]
                spec[i0 + di, here, :block] = rr - ii
                spec[i0 + di, here, block:] = ss - rr - ii
        return carry

    lax.fori_loop(0, width // 8, some_channels, 0, unroll=True)
    whole = spec[...].reshape(count * width, 2 * block)
    high = whole.astype(BF16)
    low = (whole - high.astype(F32)).astype(BF16)
    wide = (
        jnp.dot(high, inv_ref[0], preferred_element_type=F32)
        + jnp.dot(low, inv_ref[0], preferred_element_type=F32)
        + jnp.dot(high, inv_ref[1], preferred_element_type=F32)
    )
    head = wide[:, :block].reshape(count, width, block)
    tail = wide[:, block:].reshape(count, width, block)
    out_ref[0] = head[0].astype(BF16)
    out_ref[1:] = (head[1:] + tail[:-1]).astype(BF16)


def gate_kernel(conv_ref, values_ref, gates_ref, gain_ref, out_ref):
    peers, width, block = conv_ref.shape
    convolved = conv_ref[...].reshape(peers * width, block).astype(F32).T
    direct = gain_ref[...] * values_ref[...].astype(F32)
    out_ref[...] = (gates_ref[...].astype(F32) * (convolved + direct)).astype(BF16)


def place_kernel(place_ref, own_a, own_b, got_a, out_ref):
    mine = place_ref[0]
    seqs, block, _ = out_ref.shape
    odd = mine % 2
    even_chip = mine + odd
    odd_chip = even_chip - 1
    near_mine = jnp.where(odd == 1, odd_chip - 1, even_chip)
    near_theirs = jnp.where(odd == 1, even_chip, odd_chip - 1)
    far_mine = jnp.where(odd == 1, mine - 3, mine + 2)
    for part, first, second in (
        (own_a, near_mine, near_mine + 1),
        (got_a, near_theirs, near_theirs + 1),
        (own_b, far_mine, far_mine + 1),
    ):
        out_ref[lax.rem(first + 2 * seqs, seqs)] = part[:block]
        out_ref[lax.rem(second + 2 * seqs, seqs)] = part[block:]


def place_most(place, own_a, own_b, got_a, seqs, block):
    return pl.pallas_call(
        place_kernel,
        in_specs=[pl.BlockSpec(memory_space=pltpu.SMEM)] + [pl.BlockSpec(memory_space=pltpu.VMEM)] * 3,
        out_shape=jax.ShapeDtypeStruct((seqs, block, own_a.shape[1]), BF16),
        compiler_params=pltpu.CompilerParams(vmem_limit_bytes=4 * 2**20),
        name="place",
    )(place, own_a, own_b, got_a)


def body(values, gates, skip_gain, filter_taps, out_weight):
    block, chans = values.shape[1:]
    peers = lax.axis_size("ctx")
    width = chans // peers
    values, gates = values[0], gates[0]
    forward, inverse = dft_tables(block)
    small = pltpu.CompilerParams(vmem_limit_bytes=8 * 2**20)
    count = lax.axis_size("rep")
    mine, core = lax.axis_index("rep"), lax.axis_index("fsdp")
    place = jnp.stack([mine, core]).astype(jnp.int32)
    row_pairs = [[i, i + 1] for i in range(0, count, 2)]
    column_swap = [(i, (i - 1 if i % 2 == 0 else i + 1) % count) for i in range(count)]
    onward = [(i, (i - 2 if i % 2 == 0 else i + 2) % count) for i in range(count)]
    partner_weight = lax.ppermute(out_weight, "rep", column_swap)

    packed = pl.pallas_call(
        pack_kernel,
        in_specs=[pl.BlockSpec(memory_space=pl.ANY)] * 2,
        out_shape=jax.ShapeDtypeStruct((peers, 2 * width, block), BF16),
        scratch_shapes=[
            pltpu.VMEM(values.shape, BF16),
            pltpu.VMEM(filter_taps.shape, F32),
            pltpu.SemaphoreType.DMA((2,)),
        ],
        compiler_params=pltpu.CompilerParams(vmem_limit_bytes=60 * 2**20),
        name="pack",
    )(values, filter_taps)
    turned = lax.all_to_all(packed, "ctx", split_axis=0, concat_axis=0, tiled=True)
    convolved = pl.pallas_call(
        conv_kernel,
        out_shape=jax.ShapeDtypeStruct((peers, width, block), BF16),
        scratch_shapes=[
            pltpu.VMEM((3, peers, width, block), F32),
            pltpu.VMEM((3, peers, width, block), F32),
            pltpu.VMEM((peers, width, 2 * block), F32),
        ],
        compiler_params=pltpu.CompilerParams(vmem_limit_bytes=20 * 2**20),
        name="conv",
    )(turned, forward, inverse)
    back = lax.all_to_all(convolved, "ctx", split_axis=0, concat_axis=0, tiled=True)
    mixed = pl.pallas_call(
        gate_kernel,
        out_shape=jax.ShapeDtypeStruct((block, chans), BF16),
        compiler_params=small,
        name="gate",
    )(back, values, gates, skip_gain[None, :])

    keep = out_weight.shape[1] // 2
    weights = jnp.concatenate(
        [
            lax.dynamic_slice_in_dim(w, side * keep, keep, 1)
            for side in (core, 1 - core)
            for w in (out_weight, partner_weight)
        ],
        axis=1,
    )
    near = lax.all_gather(mixed, "rep", axis=0, axis_index_groups=row_pairs)
    far = lax.ppermute(near, "rep", onward)

    def columns(product):
        came = lax.all_gather(product[:, 2 * keep :].astype(BF16), "fsdp", axis=0)
        total = product[:, : 2 * keep] + lax.dynamic_index_in_dim(came, 1 - core, 0, False).astype(F32)
        total = total.astype(BF16)
        return total[:, :keep], lax.ppermute(total[:, keep:], "rep", column_swap)

    own_a, got_a = columns(
        jnp.dot(near.reshape(2 * block, chans), weights, preferred_element_type=F32)
    )
    far, own_a = lax.optimization_barrier((far, own_a))
    far_rows = far.reshape(2 * block, chans)

    def one_block(first):
        here, away = (weights[:, at : at + keep] for at in (first, first + 2 * keep))
        sent = jnp.dot(far_rows, away, preferred_element_type=F32).astype(BF16)
        came = lax.all_gather(sent, "fsdp", axis=0)
        kept = jnp.dot(far_rows, here, preferred_element_type=F32)
        return (kept + lax.dynamic_index_in_dim(came, 1 - core, 0, False).astype(F32)).astype(BF16)

    got_b = lax.ppermute(one_block(keep), "rep", column_swap)
    own_b = one_block(0)
    out = place_most(place, own_a, own_b, got_a, count, block)
    low = jnp.where(mine % 2 == 1, mine + 3, mine - 4 + count) % count
    return lax.dynamic_update_slice(out, got_b.reshape(2, block, keep), (low, 0, 0))


def solution(mesh):
    return jax.shard_map(
        body,
        mesh=mesh,
        in_specs=(
            P("rep", "ctx", "fsdp"),
            P("rep", "ctx", "fsdp"),
            P("fsdp"),
            P("ctx", "fsdp"),
            P("fsdp", "rep"),
        ),
        out_specs=P(None, "ctx", ("rep", "fsdp")),
        check_vma=False,
    )
```
